32 devices in a mesh: groups: 2 (over y), param: 8 (over z, x), ex: 2 (over core).
Axes of the slice: x: 2, y: 2, z: 4, core: 2. Of those that a mesh axis runs over, the one named last changes fastest.
Arguments:
- g_train: bfloat16 [2048, 65536], P(('groups', 'ex'), 'param'), parts along dimension 0, may hold values from -6 to 6
- g_target: bfloat16 [1024, 65536], P(('groups', 'ex'), 'param'), parts along dimension 0, may hold values from -6 to 6
- projection: bfloat16 [65536, 4096], P('param'), may hold values from -0.03125 to 0.03125
- kernel_inv: bfloat16 [8192, 4096], P('groups', 'param'), parts along dimension 0, may hold values from -0.09375 to 0.09375
Outputs:
- scores: float32 [2048, 512], P(('groups', 'ex'), 'param'), parts along dimension 0
The draws below stay inside these ranges and needn't reach their ends.
There are 2 independent parts, one for each index of `groups`. The reference program is written for one: setup_inputs(seed, part) draws one part's arguments, and reference() takes and returns one part's arrays. A program takes and returns all parts, laid end to end along the dimension named above; an argument that names none is the same for every part. Nothing has to cross between parts.
All inputs are finite; a program needn't handle non-finite values.
Results may differ from the reference program's by a relative error of at most 0.0041.
Values may be sent and summed in bfloat16 or wider, within the bound.
No kernel may reach another device: no remote copies, remote signals or barrier semaphores. Data moves between devices by JAX's collectives and lax.ppermute only.
A program may use at most 192 MiB of HBM per device.

```python
import math
import jax
import jax.numpy as jnp
from jax import lax

P_SIZE = 65536
K = 4096
NTR = 1024
NTG = 512


def raised(result, key, source, target, blocks, factor):
    def block_of(position):
        return (jnp.arange(result.shape[position]) // (result.shape[position] // blocks)).reshape((-1,) + (1,) * (result.ndim - 1 - position))

    near = jax.random.permutation(key, blocks)[block_of(target)]
    second = (block_of(target) + blocks // 2) % blocks
    return jnp.where((block_of(source) == near) | (block_of(source) == second), factor * result, result)


def level_of(rng, extent, shards, low, largest):
    def one(position, parts):
        heights = jax.random.uniform(jax.random.fold_in(jax.random.fold_in(rng, 6), position), (parts,), jnp.float32, low / len(shards), largest / len(shards))
        return jnp.repeat(jnp.exp(heights), extent[position] // parts).reshape((-1,) + (1,) * (len(extent) - position - 1))

    loudness = one(*shards[0])
    for cut in shards[1:]:
        loudness = loudness * one(*cut)
    return loudness


def bell_draw(stream_key, extent, width, limit, pieces=(), held_as=jnp.bfloat16):
    array = width * jax.random.normal(stream_key, extent, jnp.float32)
    if pieces:
        array = array * level_of(stream_key, extent, pieces, -0.22, 0.18)
    return jnp.clip(array, -limit, limit).astype(held_as)


def bell_draw_with(stream_key, extent, scale, most, pieces, heavy, dtype=jnp.bfloat16):
    drawn = scale * jax.random.normal(stream_key, extent, jnp.float32)
    if pieces:
        drawn = drawn * level_of(stream_key, extent, pieces, -0.22, 0.18)
    return jnp.clip(raised(drawn, jax.random.fold_in(stream_key, 3), *heavy), -most, most).astype(dtype)


def setup_inputs(seed: int = 0, part: int = 0) -> dict:
    key_list = jax.random.split(jax.random.key(seed), 5)
    part_keys = jax.random.split(jax.random.fold_in(key_list[4], part), 5)
    g_train = bell_draw(part_keys[0], (NTR, P_SIZE), 1.0, 6.0, ((0, 2), (1, 8)))
    g_target = bell_draw(part_keys[1], (NTG, P_SIZE), 1.0, 6.0, ((0, 2), (1, 8)))
    projection = bell_draw_with(key_list[2], (P_SIZE, K), P_SIZE ** -0.5, 0.03125, ((0, 8),), (0, 1, 8, 2.0))
    kernel_inv = bell_draw(part_keys[3], (K, K), K ** -0.5, 0.09375, ((1, 8),))
    return {"g_train": g_train, "g_target": g_target, "projection": projection, "kernel_inv": kernel_inv}


def reference(g_train, g_target, projection, kernel_inv):
    train_feat = jnp.dot(g_train, projection, preferred_element_type=jnp.float32)
    target_feat = jnp.dot(g_target, projection, preferred_element_type=jnp.float32).astype(jnp.bfloat16)
    folded = jnp.dot(target_feat, kernel_inv, preferred_element_type=jnp.float32).astype(jnp.bfloat16)
    scores = jnp.dot(train_feat, folded.astype(jnp.float32).T, precision=lax.Precision.HIGHEST)
    return scores * (1.0 / math.sqrt(K))
```

```python
import math

import jax
import jax.numpy as jnp
from jax import lax
from jax.experimental import pallas as pl
from jax.experimental.pallas import tpu as pltpu
from jax.sharding import PartitionSpec as P

BOTH = ("param", "ex")
SCALE_ROWS = 16


def hop_order(bits):
    low = max(1, bits // 3)
    plain = list(range(bits))
    return [plain, plain[low : 2 * low] + plain[:low] + plain[2 * low :]]


class Cube:
    def __init__(self, n, cores):
        self.n = n
        self.bits = n.bit_length() - 1
        two = hop_order(self.bits)
        self.orders = [two[e % 2] for e in range(cores)]
        self.me = lax.axis_index("param")
        self.core = lax.axis_index("ex")
        self.perms = [
            [
                (p * cores + e, (p ^ (1 << self.orders[e][h])) * cores + e)
                for p in range(n)
                for e in range(cores)
            ]
            for h in range(self.bits)
        ]
        masks = [
            [
                sum(((i >> (self.bits - 1 - h)) & 1) << self.orders[e][h] for h in range(self.bits))
                for i in range(n)
            ]
            for e in range(cores)
        ]
        self.blocks = jnp.bitwise_xor(self.me, jnp.array(masks, jnp.int32)[self.core])
        table = jnp.array(self.orders, jnp.int32)[self.core]
        self.bit = [jnp.bitwise_and(jnp.right_shift(self.me, table[h]), 1) for h in range(self.bits)]

    def swap(self, value, hop):
        return lax.ppermute(value, BOTH, self.perms[hop])


def pow2(k):
    return jnp.exp2(k)


def exponent(top):
    k = jnp.ceil(jnp.log2(jnp.maximum(top, 1e-37)))
    return jnp.clip(k, -110.0, 100.0)


def pack(value, k):
    body = (value * pow2(14.0 - k)).astype(jnp.float16)
    tail = jnp.full((SCALE_ROWS, value.shape[1]), k, jnp.float16)
    return jnp.concatenate([body, tail], axis=0)


def unpack(message):
    rows = message.shape[0] - SCALE_ROWS
    k = message[rows, 0].astype(jnp.float32)
    return message[:rows].astype(jnp.float32) * pow2(k - 14.0), k


def reduce_columns(cube, value):
    k = exponent(jnp.max(jnp.abs(value)))
    for hop in range(cube.bits):
        half = value.shape[1] // 2
        first, second = value[:, :half], value[:, half:]
        low = cube.bit[hop] == 0
        got, other = unpack(cube.swap(pack(jnp.where(low, second, first), k), hop))
        value = jnp.where(low, first, second) + got
        k = jnp.maximum(k, other) + 1.0
    return value


def gather_columns(cube, value):
    for hop in reversed(range(cube.bits)):
        got = cube.swap(value, hop)
        low = cube.bit[hop] == 0
        value = jnp.where(
            low, jnp.concatenate([value, got], axis=1), jnp.concatenate([got, value], axis=1)
        )
    return value


def score_kernel(parts, scale, blocks_ref, *refs):
    projection, (folded, own, other, out_own, out_other) = refs[:parts], refs[parts:]
    width = projection[0].shape[1]
    products = None
    for i in range(parts):
        part = lax.dot_general(
            projection[i][...],
            folded[:, i * width : (i + 1) * width],
            (((1,), (1,)), ((), ())),
            preferred_element_type=jnp.float32,
        )
        products = part if products is None else products + part
    weights = (products * scale).astype(jnp.bfloat16)

    @pl.when(pl.program_id(0) == 0)
    def _():
        out_own[...] = jnp.zeros_like(out_own)
        out_other[...] = jnp.zeros_like(out_other)

    for grad, out in ((own, out_own), (other, out_other)):
        out[...] += lax.dot_general(
            weights, grad[...], (((0,), (1,)), ((), ())), preferred_element_type=jnp.float32
        )


def score_terms(projection, folded, own, other, blocks, parts, scale):
    rows, targets, train = projection.shape[0], folded.shape[0], own.shape[0]
    step = min(512, rows)
    width = folded.shape[1] // parts

    def column(i):
        return pl.BlockSpec((step, width), lambda r, b: (r, b[i]))

    grad = pl.BlockSpec((train, step), lambda r, b: (0, r))
    out = pl.BlockSpec((targets, train), lambda r, b: (0, 0))
    shape = jax.ShapeDtypeStruct((targets, train), jnp.float32)
    flops = 2 * rows * targets * (folded.shape[1] + 2 * train)
    return pl.pallas_call(
        lambda *refs: score_kernel(parts, scale, *refs),
        grid_spec=pltpu.PrefetchScalarGridSpec(
            num_scalar_prefetch=1,
            grid=(rows // step,),
            in_specs=[column(i) for i in range(parts)]
            + [pl.BlockSpec(folded.shape, lambda r, b: (0, 0)), grad, grad],
            out_specs=[out, out],
        ),
        out_shape=[shape, shape],
        compiler_params=pltpu.CompilerParams(vmem_limit_bytes=48 * 2**20),
        cost_estimate=pl.CostEstimate(
            flops=flops,
            bytes_accessed=2 * rows * (folded.shape[1] + 2 * train),
            transcendentals=0,
        ),
    )(blocks, *([projection] * parts), folded, own, other)


def on_device(n, cores, g_train, g_target, projection, kernel_inv):
    cube = Cube(n, cores)
    features = projection.shape[1]
    scale = 1.0 / math.sqrt(features)
    swap_cores = [(e, e ^ 1) for e in range(cores)]
    g_other = lax.ppermute(g_train, "ex", swap_cores)

    chunks = 2
    width = features // chunks
    summed = None
    for c in range(chunks):
        part = jnp.dot(
            g_target, projection[:, c * width : (c + 1) * width], preferred_element_type=jnp.float32
        )
        target = gather_columns(cube, reduce_columns(cube, part).astype(jnp.bfloat16))
        term = jnp.dot(
            target, kernel_inv[c * width : (c + 1) * width], preferred_element_type=jnp.float32
        )
        summed = term if summed is None else summed + term
    pieces = summed.astype(jnp.bfloat16)

    for hop in reversed(range(1, cube.bits)):
        pieces = jnp.concatenate([pieces, cube.swap(pieces, hop)], axis=1)
    rest = cube.swap(pieces, 0)
    half = n // 2
    if (features // n) % 128 == 0:
        first = score_terms(projection, pieces, g_train, g_other, cube.blocks[:half], half, scale)
        second = score_terms(projection, rest, g_train, g_other, cube.blocks[half:], half, scale)
        own, other = first[0] + second[0], first[1] + second[1]
    else:
        stacked = jnp.concatenate([pieces, rest], axis=1).reshape(pieces.shape[0], n, -1)
        folded = jnp.take(stacked, jnp.argsort(cube.blocks), axis=1).reshape(pieces.shape[0], -1)
        own, other = score_terms(
            projection, folded, g_train, g_other, jnp.zeros((1,), jnp.int32), 1, scale
        )

    got = lax.ppermute(other, "ex", swap_cores)
    swapped = cube.core == 1
    value = jnp.concatenate([jnp.where(swapped, got, own), jnp.where(swapped, own, got)], axis=0)
    train = value.shape[1]
    value = value.reshape(n, -1, train)
    for hop in range(cube.bits):
        keeps, sends = [], []
        for e in range(2):
            left = sorted(cube.orders[e % cores][hop:])
            below = left.index(cube.orders[e % cores][hop])
            view = value.reshape(-1, 2, 2**below, value.shape[1], train)
            low = cube.bit[hop] == 0
            keeps.append(jnp.where(low, view[:, 0], view[:, 1]).reshape(-1, value.shape[1], train))
            sends.append(jnp.where(low, view[:, 1], view[:, 0]).reshape(-1, value.shape[1], train))
        keep = jnp.where(cube.core % 2 == 0, keeps[0], keeps[1])
        send = jnp.where(cube.core % 2 == 0, sends[0], sends[1])
        value = keep + cube.swap(send, hop)
    return value.reshape(-1, train).T


def solution(mesh):
    placed = (
        P(("groups", "ex"), "param"),
        P(("groups", "ex"), "param"),
        P("param", None),
        P("groups", "param"),
    )
    n, cores = mesh.shape["param"], mesh.shape["ex"]
    return jax.shard_map(
        lambda *args: on_device(n, cores, *args),
        mesh=mesh,
        in_specs=placed,
        out_specs=P(("groups", "ex"), "param"),
        check_vma=False,
    )
```

```python
import functools
import math

import jax
import jax.numpy as jnp
from jax import lax
from jax.experimental import pallas as pl
from jax.experimental.pallas import tpu as pltpu
from jax.sharding import PartitionSpec as P

BOTH = ("param", "ex")
SCALE_ROWS = 16
F32 = jnp.float32
BF16 = jnp.bfloat16


def turn(order, low):
    return order[low : 2 * low] + order[:low] + order[2 * low :]


class Cube:
    def __init__(self, n, orders):
        cores = len(orders)
        self.n, self.orders = n, orders
        self.bits = n.bit_length() - 1
        self.perms = [
            [
                (p * cores + e, (p ^ (1 << self.orders[e][h])) * cores + e)
                for p in range(n)
                for e in range(cores)
            ]
            for h in range(self.bits)
        ]
        masks = [
            [
                sum(((i >> (self.bits - 1 - h)) & 1) << self.orders[e][h] for h in range(self.bits))
                for i in range(n)
            ]
            for e in range(cores)
        ]
        self.core = lax.axis_index("ex")
        mine = jnp.array(masks, jnp.int32)[self.core]
        self.blocks = jnp.bitwise_xor(lax.axis_index("param"), mine)

    def swap(self, value, hop):
        return lax.ppermute(value, BOTH, self.perms[hop])


def product_kernel(with_top, blocks_ref, g_ref, p_ref, *refs):
    outs = refs[len(refs) - 1 - with_top :]
    value = jnp.dot(g_ref[...], p_ref[...], preferred_element_type=F32)
    outs[0][...] = value.astype(outs[0].dtype)
    if with_top:
        outs[1][...] = jnp.broadcast_to(jnp.max(jnp.abs(value), axis=0, keepdims=True), outs[1].shape)


def product(g, projection, blocks, width, dtype, with_top=False, after=()):
    rows, depth = g.shape
    count = blocks.shape[0]
    out_shape = [jax.ShapeDtypeStruct((rows, count * width), dtype)]
    out_specs = [pl.BlockSpec((rows, width), lambda i, b: (0, i))]
    if with_top:
        out_shape.append(jax.ShapeDtypeStruct((8, count * width), F32))
        out_specs.append(pl.BlockSpec((8, width), lambda i, b: (0, i)))
    return pl.pallas_call(
        functools.partial(product_kernel, with_top),
        grid_spec=pltpu.PrefetchScalarGridSpec(
            num_scalar_prefetch=1,
            grid=(count,),
            in_specs=[
                pl.BlockSpec(memory_space=pltpu.VMEM),
                pl.BlockSpec((depth, width), lambda i, b: (0, b[i])),
            ]
            + [pl.BlockSpec(memory_space=pl.ANY)] * len(after),
            out_specs=out_specs,
        ),
        out_shape=out_shape,
        compiler_params=pltpu.CompilerParams(vmem_limit_bytes=28 * 2**20),
        cost_estimate=pl.CostEstimate(
            flops=2 * rows * depth * count * width,
            bytes_accessed=2 * depth * count * width,
            transcendentals=0,
        ),
    )(blocks, g, projection, *after)


def fold_kernel(blocks_ref, target_ref, inverse_ref, out_ref):
    count = blocks_ref.shape[0]
    width = target_ref.shape[1] // count
    total = None
    for i in range(count):
        rows = pl.ds(pl.multiple_of(blocks_ref[i] * width, width), width)
        term = jnp.dot(
            target_ref[:, i * width : (i + 1) * width],
            inverse_ref[rows, :],
            preferred_element_type=F32,
        )
        total = term if total is None else total + term
    out_ref[...] = total.astype(out_ref.dtype)


def fold(target, inverse, blocks):
    rows, columns = target.shape[0], inverse.shape[1]
    vmem = pl.BlockSpec(memory_space=pltpu.VMEM)
    return pl.pallas_call(
        fold_kernel,
        in_specs=[pl.BlockSpec(memory_space=pltpu.SMEM), vmem, vmem],
        out_specs=vmem,
        out_shape=jax.ShapeDtypeStruct((rows, columns), BF16),
        compiler_params=pltpu.CompilerParams(vmem_limit_bytes=16 * 2**20),
        cost_estimate=pl.CostEstimate(
            flops=2 * rows * target.shape[1] * columns,
            bytes_accessed=2 * target.shape[1] * columns,
            transcendentals=0,
        ),
    )(blocks, target, inverse)


def score_kernel(scale, count, order_ref, own_ref, got_ref, *refs):
    train, (keep_ref, send_ref, folded_ref, placed_ref) = refs[:-4], refs[-4:]
    rows = own_ref.shape[0]
    folded_ref[:rows] = own_ref[...]
    folded_ref[rows:] = got_ref[...]
    height = 2 * rows // count
    for i in range(count):
        source = pl.ds(pl.multiple_of(order_ref[i] * height, height), height)
        placed_ref[i * height : (i + 1) * height] = folded_ref[source, :]
    folded = placed_ref[...]
    width = train[0].shape[1]
    total = None
    for c in range(len(train) // 2):
        value = train[2 * c][...] + train[2 * c + 1][...].astype(F32)
        high = value.astype(BF16)
        low = (value - high.astype(F32)).astype(BF16)
        for part in (high, low):
            term = lax.dot_general(
                folded[:, c * width : (c + 1) * width],
                part,
                (((1,), (1,)), ((), ())),
                preferred_element_type=F32,
            )
            total = term if total is None else total + term
    total = total * scale
    keep_ref[...] = total[:rows]
    send_ref[...] = total[rows:]


def score_terms(own, got, train, order, scale):
    rows, columns = own.shape
    vmem = pl.BlockSpec(memory_space=pltpu.VMEM)
    shape = jax.ShapeDtypeStruct((rows, train[0].shape[0]), F32)
    return pl.pallas_call(
        functools.partial(score_kernel, scale, order.shape[0]),
        in_specs=[pl.BlockSpec(memory_space=pltpu.SMEM)] + [vmem] * (2 + len(train)),
        out_specs=[vmem, vmem],
        out_shape=[shape, shape],
        scratch_shapes=[pltpu.VMEM((2 * rows, columns), BF16)] * 2,
        compiler_params=pltpu.CompilerParams(vmem_limit_bytes=16 * 2**20),
    )(order, own, got, *train)


def exponent(top):
    k = jnp.ceil(jnp.log2(jnp.maximum(top, 1e-37)))
    return jnp.clip(k, -110.0, 100.0)


def pack(value, k):
    tail = jnp.broadcast_to(k, (SCALE_ROWS, k.shape[1]))
    return jnp.concatenate([value * jnp.exp2(14.0 - k), tail], axis=0).astype(jnp.float16)


def unpack(message):
    rows = message.shape[0] - SCALE_ROWS
    k = message[rows:].astype(F32)[:1]
    return message[:rows].astype(F32) * jnp.exp2(k - 14.0), k


def halves(value):
    middle = value.shape[1] // 2
    return value[:, :middle], value[:, middle:]


def on_device(n, cores, g_train, g_target, projection, kernel_inv):
    plain = list(range(n.bit_length() - 1))
    low = max(1, len(plain) // 3)
    cube = Cube(n, [plain, turn(plain, low)])
    train_cube = Cube(n, [plain, plain[:low] + plain[:low - 1:-1]])
    last_cube = Cube(n, [plain, plain[low:] + plain[:low]])
    features = projection.shape[1]
    width = features // n
    scale = 1.0 / math.sqrt(features)
    swap_cores = [(e, e ^ 1) for e in range(cores)]
    half = n // 2
    chunks = 2
    pieces = [train_cube.blocks * chunks + c for c in range(chunks)]

    def train_product(c, sends, after):
        blocks = pieces[c][half:] if sends else pieces[c][:half]
        return product(g_train, projection, blocks, width // chunks, BF16, after=after)[0]

    value, top = product(g_target, projection, cube.blocks[half:], width, F32, with_top=True)
    message = pack(value, exponent(top[:1]))
    value, top = product(
        g_target, projection, cube.blocks[:half], width, F32, with_top=True, after=(value,)
    )
    k = exponent(top[:1])

    def receive(hop, value, k):
        got, other = unpack(cube.swap(message, hop))
        return value + got, jnp.maximum(k, other) + 1.0

    sends, keeps, moving = [], [], [None, None]
    value, k = receive(0, value, k)
    for hop in range(1, cube.bits):
        (keep, onward), (keep_k, onward_k) = halves(value), halves(k)
        message = pack(onward, onward_k)
        if hop == 1:
            sends.append(train_product(0, True, (value,)))
        elif hop == 2:
            sends.append(train_product(1, True, (value, sends[0])))
        value, k = keep, keep_k
        value, k = receive(hop, value, k)
    target = value.astype(BF16)
    keeps.append(train_product(0, False, (target, sends[1])))

    def train_hop(c, hop):
        if hop == 0:
            return keeps[c].astype(F32) + train_cube.swap(sends[c], 0).astype(F32)
        keep, send = halves(moving[c])
        return keep + train_cube.swap(send.astype(BF16), hop).astype(F32)

    for hop in reversed(range(cube.bits)):
        got = cube.swap(target, hop)
        target = jnp.concatenate([target, got], axis=1)
        if hop == cube.bits - 1:
            keeps.append(train_product(1, False, (target, keeps[0])))
    own = fold(target, kernel_inv, cube.blocks)
    got = lax.ppermute(own, "ex", swap_cores)

    train = []
    for c in range(chunks):
        for hop in range(cube.bits - 1):
            moving[c] = train_hop(c, hop)
        keep, send = halves(moving[c])
        train += [keep, train_cube.swap(send.astype(BF16), cube.bits - 1)]

    order = jnp.bitwise_xor(last_cube.blocks, half * cube.core)
    keep, send = score_terms(own, got, train, order, scale)
    for hop in range(cube.bits):
        value = keep + last_cube.swap(send.astype(BF16), hop).astype(F32)
        rows = value.shape[0] // 2
        keep, send = value[:rows], value[rows:]
    return value.T


def plain_on_device(g_train, g_target, projection, kernel_inv):
    factor = 1.0 / math.sqrt(projection.shape[1])
    target_part = jnp.dot(g_target, projection, preferred_element_type=F32)
    target_feat = lax.psum_scatter(target_part, "param", scatter_dimension=1, tiled=True)
    target_full = lax.all_gather(target_feat.astype(BF16), "param", axis=1, tiled=True)
    every_target = lax.all_gather(target_full, "ex", axis=0, tiled=True)
    folded = jnp.dot(every_target, kernel_inv, preferred_element_type=F32).astype(BF16)
    train_part = jnp.dot(g_train, projection, preferred_element_type=F32)
    train_feat = lax.psum_scatter(train_part, "param", scatter_dimension=1, tiled=True)
    terms = jnp.dot(train_feat, folded.astype(F32).T, precision=lax.Precision.HIGHEST)
    return lax.psum_scatter(terms * factor, "param", scatter_dimension=1, tiled=True)


def solution(mesh):
    placed = (
        P(("groups", "ex"), "param"),
        P(("groups", "ex"), "param"),
        P("param", None),
        P("groups", "param"),
    )
    n, cores = mesh.shape["param"], mesh.shape["ex"]

    def body(g_train, g_target, projection, kernel_inv):
        whole_blocks = (projection.shape[1] // n) % 256 == 0 and cores == 2 and n & (n - 1) == 0
        form = functools.partial(on_device, n, cores) if whole_blocks else plain_on_device
        return form(g_train, g_target, projection, kernel_inv)

    return jax.shard_map(
        body,
        mesh=mesh,
        in_specs=placed,
        out_specs=P(("groups", "ex"), "param"),
        check_vma=False,
    )
```

```python
import functools
import math

import jax
import jax.numpy as jnp
from jax import lax
from jax.experimental import pallas as pl
from jax.experimental.pallas import tpu as pltpu
from jax.sharding import PartitionSpec as P

BOTH = ("param", "ex")
SCALE_ROWS = 16
F32 = jnp.float32
BF16 = jnp.bfloat16
LIGHT = pl.CostEstimate(flops=1024, bytes_accessed=1024, transcendentals=0)


class Cube:
    def __init__(self, n, orders):
        cores = len(orders)
        self.n, self.orders = n, orders
        self.bits = n.bit_length() - 1
        self.perms = [
            [
                (p * cores + e, (p ^ (1 << self.orders[e][h])) * cores + e)
                for p in range(n)
                for e in range(cores)
            ]
            for h in range(self.bits)
        ]
        self.masks = [
            [
                sum(((i >> (self.bits - 1 - h)) & 1) << self.orders[e][h] for h in range(self.bits))
                for i in range(n)
            ]
            for e in range(cores)
        ]
        self.core = lax.axis_index("ex")
        mine = jnp.array(self.masks, jnp.int32)[self.core]
        self.blocks = jnp.bitwise_xor(lax.axis_index("param"), mine)

    def partners(self, e, i):
        return [p ^ self.masks[e][i] for p in range(self.n)]

    def swap(self, value, hop):
        return lax.ppermute(value, BOTH, self.perms[hop])


def product_kernel(with_top, blocks_ref, g_ref, p_ref, *refs):
    outs = refs[len(refs) - 1 - with_top :]
    value = jnp.dot(g_ref[...], p_ref[...], preferred_element_type=F32)
    outs[0][...] = value.astype(outs[0].dtype)
    if with_top:
        outs[1][...] = jnp.broadcast_to(jnp.max(jnp.abs(value), axis=0, keepdims=True), outs[1].shape)


def product(g, projection, blocks, width, dtype, with_top=False, after=()):
    rows, depth = g.shape
    count = blocks.shape[0]
    out_shape = [jax.ShapeDtypeStruct((rows, count * width), dtype)]
    out_specs = [pl.BlockSpec((rows, width), lambda i, b: (0, i))]
    if with_top:
        out_shape.append(jax.ShapeDtypeStruct((8, count * width), F32))
        out_specs.append(pl.BlockSpec((8, width), lambda i, b: (0, i)))
    return pl.pallas_call(
        functools.partial(product_kernel, with_top),
        grid_spec=pltpu.PrefetchScalarGridSpec(
            num_scalar_prefetch=1,
            grid=(count,),
            in_specs=[
                pl.BlockSpec(memory_space=pltpu.VMEM),
                pl.BlockSpec((depth, width), lambda i, b: (0, b[i])),
            ]
            + [pl.BlockSpec(memory_space=pl.ANY)] * len(after),
            out_specs=out_specs,
        ),
        out_shape=out_shape,
        compiler_params=pltpu.CompilerParams(vmem_limit_bytes=28 * 2**20),
        cost_estimate=LIGHT,
    )(blocks, g, projection, *after)


def fold_kernel(blocks_ref, target_ref, inverse_ref, out_ref):
    count = blocks_ref.shape[0]
    width = target_ref.shape[1] // count
    total = None
    for i in range(count):
        rows = pl.ds(pl.multiple_of(blocks_ref[i] * width, width), width)
        term = jnp.dot(
            target_ref[:, i * width : (i + 1) * width],
            inverse_ref[rows, :],
            preferred_element_type=F32,
        )
        total = term if total is None else total + term
    out_ref[...] = total.astype(out_ref.dtype)


def fold(target, inverse, blocks):
    rows, columns = target.shape[0], inverse.shape[1]
    vmem = pl.BlockSpec(memory_space=pltpu.VMEM)
    return pl.pallas_call(
        fold_kernel,
        in_specs=[pl.BlockSpec(memory_space=pltpu.SMEM), vmem, vmem],
        out_specs=vmem,
        out_shape=jax.ShapeDtypeStruct((rows, columns), BF16),
        compiler_params=pltpu.CompilerParams(vmem_limit_bytes=16 * 2**20),
        cost_estimate=LIGHT,
    )(blocks, target, inverse)


def score_kernel(scale, count, order_ref, own_ref, got_ref, *refs):
    train, outs, (folded_ref, placed_ref) = refs[: -2 - count], refs[-2 - count : -2], refs[-2:]
    rows = own_ref.shape[0]
    folded_ref[:rows] = own_ref[...]
    folded_ref[rows:] = got_ref[...]
    height = 2 * rows // count
    for i in range(count):
        source = pl.ds(pl.multiple_of(order_ref[i] * height, height), height)
        placed_ref[i * height : (i + 1) * height] = folded_ref[source, :]
    folded = placed_ref[...]
    width = train[0].shape[1]
    total = None
    for c in range(len(train) // 2):
        value = train[2 * c][...] + train[2 * c + 1][...].astype(F32)
        high = value.astype(BF16)
        low = (value - high.astype(F32)).astype(BF16)
        for part in (high, low):
            term = lax.dot_general(
                folded[:, c * width : (c + 1) * width],
                part,
                (((1,), (1,)), ((), ())),
                preferred_element_type=F32,
            )
            total = term if total is None else total + term
    total = total * scale
    for i in range(count):
        outs[i][...] = total[i * height : (i + 1) * height].astype(outs[i].dtype)


def score_terms(own, got, train, order, scale):
    rows, columns = own.shape
    count = order.shape[0]
    vmem = pl.BlockSpec(memory_space=pltpu.VMEM)
    shape = (2 * rows // count, train[0].shape[0])
    return pl.pallas_call(
        functools.partial(score_kernel, scale, count),
        in_specs=[pl.BlockSpec(memory_space=pltpu.SMEM)] + [vmem] * (2 + len(train)),
        out_specs=[vmem] * count,
        out_shape=[jax.ShapeDtypeStruct(shape, BF16 if i else F32) for i in range(count)],
        scratch_shapes=[pltpu.VMEM((2 * rows, columns), BF16)] * 2,
        cost_estimate=LIGHT,
        compiler_params=pltpu.CompilerParams(vmem_limit_bytes=16 * 2**20),
    )(order, own, got, *train)


def exponent(top):
    k = jnp.ceil(jnp.log2(jnp.maximum(top, 1e-37)))
    return jnp.clip(k, -110.0, 100.0)


def pack(value, k):
    tail = jnp.broadcast_to(k, (SCALE_ROWS, k.shape[1]))
    return jnp.concatenate([value * jnp.exp2(14.0 - k), tail], axis=0).astype(jnp.float16)


def unpack(message):
    rows = message.shape[0] - SCALE_ROWS
    k = message[rows:].astype(F32)[:1]
    return message[:rows].astype(F32) * jnp.exp2(k - 14.0), k


def halves(value):
    middle = value.shape[1] // 2
    return value[:, :middle], value[:, middle:]


STEPS = (
    "TS", "sT0", "TK", "dT0", "sT1", "Sb", "dT1", "sT2", "sB0", "Kb", "dT2", "sG0", "dB0", "sB1", "Sa", "sA0", "dG0", "sG1", "Ka", "dB1", "dG1", "sG2", "dA0", "sA1", "sB2", "dA1", "sA2", "dG2", "F", "sE0", "dE0", "dB2", "dA2", "SC",
)
AXES = {"T": ("lxh", "xhl"), "L": ("xlh", "lxh"), "A": ("lxh", "xhl"), "B": ("xhl", "lxh")}


def on_device(n, cores, g_train, g_target, projection, kernel_inv):
    features = projection.shape[1]
    width = features // n
    scale = 1.0 / math.sqrt(features)
    swap_cores = [(e, e ^ 1) for e in range(cores)]
    half = n // 2
    cubes = {unit: Cube(n, [["xlh".index(c) for c in axes] for axes in AXES[unit]]) for unit in AXES}
    hops = cubes["T"].bits
    last = []

    def ordered(*values):
        return lax.optimization_barrier((*values, *last))[: len(values)]

    def done(value):
        last[:] = [value]
        return value

    made, moving = {}, {}

    def run(step):
        kind, unit = step[0], step[1:2].upper()
        hop = int(step[2]) if len(step) == 3 else None
        if step in ("TS", "TK"):
            cube = cubes["T"]
            (blocks,) = ordered(cube.blocks[half:] if step == "TS" else cube.blocks[:half])
            value, top = product(g_target, projection, blocks, width, F32, with_top=True)
            made[step] = done(value), exponent(top[:1])
        elif step in ("Sa", "Ka", "Sb", "Kb"):
            blocks = cubes[unit].blocks * 2 + "AB".index(unit)
            blocks, dtype = (blocks[half:], BF16) if kind == "S" else (blocks[:half], F32)
            (blocks,) = ordered(blocks)
            made[step] = done(product(g_train, projection, blocks, width // 2, dtype)[0])
        elif step == "F":
            (target,) = ordered(moving["G"])
            made["F"] = done(fold(target, kernel_inv, cubes["T"].blocks))
        elif step == "SC":
            order = jnp.bitwise_xor(cubes["L"].blocks, half * cubes["L"].core)
            (order,) = ordered(order)
            train = [term for part in "AB" for term in moving[part]]
            made["SC"] = score_terms(made["F"], moving["E"], train, order, scale)
        elif unit == "T" and kind == "s":
            if hop == 0:
                kept, (value, k) = None, made["TS"]
            else:
                (keep, value), (keep_k, k) = map(halves, moving["T"])
                kept = keep, keep_k
            (value,) = ordered(value)
            message = done(pack(value, k))
            moving["T"] = kept, cubes["T"].swap(message, hop)
        elif unit == "T":
            kept, got = moving["T"]
            value, k = made["TK"] if hop == 0 else kept
            (got,) = ordered(got)
            got, other = unpack(got)
            moving["T"] = done(value + got), jnp.maximum(k, other) + 1.0
            if hop == hops - 1:
                moving["G"] = done(moving["T"][0].astype(BF16))
        elif unit == "G" and kind == "s":
            (value,) = ordered(moving["G"])
            moving["G"] = value, cubes["T"].swap(done(value), hops - 1 - hop)
        elif unit == "G":
            value, got = moving["G"]
            (got,) = ordered(got)
            moving["G"] = done(jnp.concatenate([value, got], axis=1))
        elif unit == "E" and kind == "s":
            moving["E"] = lax.ppermute(made["F"], "ex", swap_cores)
        elif unit == "E":
            pass
        elif kind == "s":
            if hop == 0:
                keep, send = None, made["S" + unit.lower()]
            else:
                keep, send = halves(moving[unit])
            (send,) = ordered(send)
            send = done(send.astype(BF16))
            moving[unit] = keep, cubes[unit].swap(send, hop)
        else:
            keep, got = moving[unit]
            keep = made["K" + unit.lower()] if hop == 0 else keep
            (got,) = ordered(got)
            if hop == hops - 1:
                moving[unit] = keep, got
            else:
                moving[unit] = done(keep + got.astype(F32))

    for step in STEPS:
        run(step)

    parts = made["SC"]
    value = parts[0]
    for i in range(1, n):
        pairs = [
            (p * cores + e, p_to * cores + e)
            for e in range(cores)
            for p, p_to in enumerate(cubes["L"].partners(e, i))
        ]
        value = value + lax.ppermute(parts[i], BOTH, pairs).astype(F32)
    return value.T


def plain_on_device(g_train, g_target, projection, kernel_inv):
    factor = 1.0 / math.sqrt(projection.shape[1])
    target_part = jnp.dot(g_target, projection, preferred_element_type=F32)
    target_feat = lax.psum_scatter(target_part, "param", scatter_dimension=1, tiled=True)
    target_full = lax.all_gather(target_feat.astype(BF16), "param", axis=1, tiled=True)
    every_target = lax.all_gather(target_full, "ex", axis=0, tiled=True)
    folded = jnp.dot(every_target, kernel_inv, preferred_element_type=F32).astype(BF16)
    train_part = jnp.dot(g_train, projection, preferred_element_type=F32)
    train_feat = lax.psum_scatter(train_part, "param", scatter_dimension=1, tiled=True)
    terms = jnp.dot(train_feat, folded.astype(F32).T, precision=lax.Precision.HIGHEST)
    return lax.psum_scatter(terms * factor, "param", scatter_dimension=1, tiled=True)


def solution(mesh):
    placed = (
        P(("groups", "ex"), "param"),
        P(("groups", "ex"), "param"),
        P("param", None),
        P("groups", "param"),
    )
    n, cores = mesh.shape["param"], mesh.shape["ex"]

    def body(g_train, g_target, projection, kernel_inv):
        whole_blocks = n == 8 and cores == 2 and (projection.shape[1] // n) % 256 == 0
        form = functools.partial(on_device, n, cores) if whole_blocks else plain_on_device
        return form(g_train, g_target, projection, kernel_inv)

    return jax.shard_map(
        body,
        mesh=mesh,
        in_specs=placed,
        out_specs=P(("groups", "ex"), "param"),
        check_vma=False,
    )
```

```python
import functools
import math

import jax
import jax.numpy as jnp
from jax import lax
from jax.experimental import pallas as pl
from jax.experimental.pallas import tpu as pltpu
from jax.sharding import PartitionSpec as P

BOTH = ("param", "ex")
SCALE_ROWS = 16
F32 = jnp.float32
BF16 = jnp.bfloat16
LIGHT = pl.CostEstimate(flops=1024, bytes_accessed=1024, transcendentals=0)


class Cube:
    def __init__(self, n, orders):
        cores = len(orders)
        self.n, self.orders = n, orders
        self.bits = n.bit_length() - 1
        self.perms = [
            [
                (p * cores + e, (p ^ (1 << self.orders[e][h])) * cores + e)
                for p in range(n)
                for e in range(cores)
            ]
            for h in range(self.bits)
        ]
        self.masks = [
            [
                sum(((i >> (self.bits - 1 - h)) & 1) << self.orders[e][h] for h in range(self.bits))
                for i in range(n)
            ]
            for e in range(cores)
        ]
        self.core = lax.axis_index("ex")
        mine = jnp.array(self.masks, jnp.int32)[self.core]
        self.blocks = jnp.bitwise_xor(lax.axis_index("param"), mine)

    def partners(self, e, i):
        return [p ^ self.masks[e][i] for p in range(self.n)]

    def swap(self, value, hop):
        return lax.ppermute(value, BOTH, self.perms[hop])


def product_kernel(with_top, blocks_ref, g_ref, p_ref, *refs):
    outs = refs[len(refs) - 1 - with_top :]
    value = jnp.dot(g_ref[...], p_ref[...], preferred_element_type=F32)
    outs[0][...] = value.astype(outs[0].dtype)
    if with_top:
        outs[1][...] = jnp.broadcast_to(jnp.max(jnp.abs(value), axis=0, keepdims=True), outs[1].shape)


def product(g, projection, blocks, width, dtype, with_top=False, after=()):
    rows, depth = g.shape
    count = blocks.shape[0]
    out_shape = [jax.ShapeDtypeStruct((rows, count * width), dtype)]
    out_specs = [pl.BlockSpec((rows, width), lambda i, b: (0, i))]
    if with_top:
        out_shape.append(jax.ShapeDtypeStruct((8, count * width), F32))
        out_specs.append(pl.BlockSpec((8, width), lambda i, b: (0, i)))
    return pl.pallas_call(
        functools.partial(product_kernel, with_top),
        grid_spec=pltpu.PrefetchScalarGridSpec(
            num_scalar_prefetch=1,
            grid=(count,),
            in_specs=[
                pl.BlockSpec(memory_space=pltpu.VMEM),
                pl.BlockSpec((depth, width), lambda i, b: (0, b[i])),
            ]
            + [pl.BlockSpec(memory_space=pl.ANY)] * len(after),
            out_specs=out_specs,
        ),
        out_shape=out_shape,
        compiler_params=pltpu.CompilerParams(vmem_limit_bytes=28 * 2**20),
        cost_estimate=LIGHT,
    )(blocks, g, projection, *after)


def fold_kernel(blocks_ref, target_ref, inverse_ref, out_ref):
    count = blocks_ref.shape[0]
    width = target_ref.shape[1] // count
    total = None
    for i in range(count):
        rows = pl.ds(pl.multiple_of(blocks_ref[i] * width, width), width)
        term = jnp.dot(
            target_ref[:, i * width : (i + 1) * width],
            inverse_ref[rows, :],
            preferred_element_type=F32,
        )
        total = term if total is None else total + term
    out_ref[...] = total.astype(out_ref.dtype)


def fold(target, inverse, blocks):
    rows, columns = target.shape[0], inverse.shape[1]
    vmem = pl.BlockSpec(memory_space=pltpu.VMEM)
    return pl.pallas_call(
        fold_kernel,
        in_specs=[pl.BlockSpec(memory_space=pltpu.SMEM), vmem, vmem],
        out_specs=vmem,
        out_shape=jax.ShapeDtypeStruct((rows, columns), BF16),
        compiler_params=pltpu.CompilerParams(vmem_limit_bytes=16 * 2**20),
        cost_estimate=LIGHT,
    )(blocks, target, inverse)


def score_kernel(scale, count, order_ref, own_ref, got_ref, *refs):
    train, outs, (folded_ref, placed_ref) = refs[: -2 - count], refs[-2 - count : -2], refs[-2:]
    rows = own_ref.shape[0]
    folded_ref[:rows] = own_ref[...]
    folded_ref[rows:] = got_ref[...]
    height = 2 * rows // count
    for i in range(count):
        source = pl.ds(pl.multiple_of(order_ref[i] * height, height), height)
        placed_ref[i * height : (i + 1) * height] = folded_ref[source, :]
    folded = placed_ref[...]
    width = train[0].shape[1]
    total = None
    for c in range(len(train) // 2):
        value = train[2 * c][...] + train[2 * c + 1][...].astype(F32)
        high = value.astype(BF16)
        low = (value - high.astype(F32)).astype(BF16)
        for part in (high, low):
            term = lax.dot_general(
                folded[:, c * width : (c + 1) * width],
                part,
                (((1,), (1,)), ((), ())),
                preferred_element_type=F32,
            )
            total = term if total is None else total + term
    total = total * scale
    for i in range(count):
        outs[i][...] = total[i * height : (i + 1) * height].astype(outs[i].dtype)


def score_terms(own, got, train, order, scale):
    rows, columns = own.shape
    count = order.shape[0]
    vmem = pl.BlockSpec(memory_space=pltpu.VMEM)
    shape = (2 * rows // count, train[0].shape[0])
    return pl.pallas_call(
        functools.partial(score_kernel, scale, count),
        in_specs=[pl.BlockSpec(memory_space=pltpu.SMEM)] + [vmem] * (2 + len(train)),
        out_specs=[vmem] * count,
        out_shape=[jax.ShapeDtypeStruct(shape, BF16 if i else F32) for i in range(count)],
        scratch_shapes=[pltpu.VMEM((2 * rows, columns), BF16)] * 2,
        cost_estimate=LIGHT,
        compiler_params=pltpu.CompilerParams(vmem_limit_bytes=16 * 2**20),
    )(order, own, got, *train)


def exponent(top):
    k = jnp.ceil(jnp.log2(jnp.maximum(top, 1e-37)))
    return jnp.clip(k, -110.0, 100.0)


def pack(value, k):
    tail = jnp.broadcast_to(k, (SCALE_ROWS, k.shape[1]))
    return jnp.concatenate([value * jnp.exp2(14.0 - k), tail], axis=0).astype(jnp.float16)


def unpack(message):
    rows = message.shape[0] - SCALE_ROWS
    k = message[rows:].astype(F32)[:1]
    return message[:rows].astype(F32) * jnp.exp2(k - 14.0), k


def halves(value):
    middle = value.shape[1] // 2
    return value[:, :middle], value[:, middle:]


STEPS = (
    "TS", "sT0", "TK", "dT0", "sT1", "Sb", "dT1", "sT2", "sB0", "Kb", "dT2", "sG0", "dB0", "sB1", "Sa", "dG0", "sA0", "sG1", "Ka", "dB1", "dG1", "sG2", "dA0", "sA1", "sB2", "dA1", "sA2", "dG2", "F", "sE0", "dE0", "dB2", "dA2", "SC",
)
AXES = {"T": ("lxh", "xhl"), "L": ("xlh", "lxh"), "A": ("lxh", "xhl"), "B": ("xhl", "lxh")}


def on_device(n, cores, g_train, g_target, projection, kernel_inv):
    features = projection.shape[1]
    width = features // n
    scale = 1.0 / math.sqrt(features)
    swap_cores = [(e, e ^ 1) for e in range(cores)]
    half = n // 2
    cubes = {unit: Cube(n, [["xlh".index(c) for c in axes] for axes in AXES[unit]]) for unit in AXES}
    hops = cubes["T"].bits
    last = []

    def ordered(*values):
        return lax.optimization_barrier((*values, *last))[: len(values)]

    def done(value):
        last[:] = [value]
        return value

    made, moving = {}, {}

    def run(step):
        kind, unit = step[0], step[1:2].upper()
        hop = int(step[2]) if len(step) == 3 else None
        if step in ("TS", "TK"):
            cube = cubes["T"]
            (blocks,) = ordered(cube.blocks[half:] if step == "TS" else cube.blocks[:half])
            value, top = product(g_target, projection, blocks, width, F32, with_top=True)
            made[step] = done(value), exponent(top[:1])
        elif step in ("Sa", "Ka", "Sb", "Kb"):
            blocks = cubes[unit].blocks * 2 + "AB".index(unit)
            blocks, dtype = (blocks[half:], BF16) if kind == "S" else (blocks[:half], F32)
            (blocks,) = ordered(blocks)
            made[step] = done(product(g_train, projection, blocks, width // 2, dtype)[0])
        elif step == "F":
            (target,) = ordered(moving["G"])
            made["F"] = done(fold(target, kernel_inv, cubes["T"].blocks))
        elif step == "SC":
            order = jnp.bitwise_xor(cubes["L"].blocks, half * cubes["L"].core)
            (order,) = ordered(order)
            train = [term for part in "AB" for term in moving[part]]
            made["SC"] = score_terms(made["F"], moving["E"], train, order, scale)
        elif unit == "T" and kind == "s":
            if hop == 0:
                kept, (value, k) = None, made["TS"]
            else:
                (keep, value), (keep_k, k) = map(halves, moving["T"])
                kept = keep, keep_k
            (value,) = ordered(value)
            message = done(pack(value, k))
            moving["T"] = kept, cubes["T"].swap(message, hop)
        elif unit == "T":
            kept, got = moving["T"]
            value, k = made["TK"] if hop == 0 else kept
            (got,) = ordered(got)
            got, other = unpack(got)
            moving["T"] = done(value + got), jnp.maximum(k, other) + 1.0
            if hop == hops - 1:
                moving["G"] = done(moving["T"][0].astype(BF16))
        elif unit == "G" and kind == "s":
            (value,) = ordered(moving["G"])
            moving["G"] = value, cubes["T"].swap(done(value), hops - 1 - hop)
        elif unit == "G":
            value, got = moving["G"]
            (got,) = ordered(got)
            moving["G"] = done(jnp.concatenate([value, got], axis=1))
        elif unit == "E" and kind == "s":
            moving["E"] = lax.ppermute(made["F"], "ex", swap_cores)
        elif unit == "E":
            pass
        elif kind == "s":
            if hop == 0:
                keep, send = None, made["S" + unit.lower()]
            else:
                keep, send = halves(moving[unit])
            (send,) = ordered(send)
            send = done(send.astype(BF16))
            moving[unit] = keep, cubes[unit].swap(send, hop)
        else:
            keep, got = moving[unit]
            keep = made["K" + unit.lower()] if hop == 0 else keep
            (got,) = ordered(got)
            if hop == hops - 1:
                moving[unit] = keep, got
            else:
                moving[unit] = done(keep + got.astype(F32))

    for step in STEPS:
        run(step)

    parts = made["SC"]
    value = parts[0]
    for i in range(1, n):
        pairs = [
            (p * cores + e, p_to * cores + e)
            for e in range(cores)
            for p, p_to in enumerate(cubes["L"].partners(e, i))
        ]
        value = value + lax.ppermute(parts[i], BOTH, pairs).astype(F32)
    return value.T


def plain_on_device(g_train, g_target, projection, kernel_inv):
    factor = 1.0 / math.sqrt(projection.shape[1])
    target_part = jnp.dot(g_target, projection, preferred_element_type=F32)
    target_feat = lax.psum_scatter(target_part, "param", scatter_dimension=1, tiled=True)
    target_full = lax.all_gather(target_feat.astype(BF16), "param", axis=1, tiled=True)
    every_target = lax.all_gather(target_full, "ex", axis=0, tiled=True)
    folded = jnp.dot(every_target, kernel_inv, preferred_element_type=F32).astype(BF16)
    train_part = jnp.dot(g_train, projection, preferred_element_type=F32)
    train_feat = lax.psum_scatter(train_part, "param", scatter_dimension=1, tiled=True)
    terms = jnp.dot(train_feat, folded.astype(F32).T, precision=lax.Precision.HIGHEST)
    return lax.psum_scatter(terms * factor, "param", scatter_dimension=1, tiled=True)


def solution(mesh):
    placed = (
        P(("groups", "ex"), "param"),
        P(("groups", "ex"), "param"),
        P("param", None),
        P("groups", "param"),
    )
    n, cores = mesh.shape["param"], mesh.shape["ex"]

    def body(g_train, g_target, projection, kernel_inv):
        whole_blocks = n == 8 and cores == 2 and (projection.shape[1] // n) % 256 == 0
        form = functools.partial(on_device, n, cores) if whole_blocks else plain_on_device
        return form(g_train, g_target, projection, kernel_inv)

    return jax.shard_map(
        body,
        mesh=mesh,
        in_specs=placed,
        out_specs=P(("groups", "ex"), "param"),
        check_vma=False,
    )
```

```python
import functools
import math

import jax
import jax.numpy as jnp
from jax import lax
from jax.experimental import pallas as pl
from jax.experimental.pallas import tpu as pltpu
from jax.sharding import PartitionSpec as P

BOTH = ("param", "ex")
SCALE_ROWS = 16
F32 = jnp.float32
BF16 = jnp.bfloat16
LIGHT = pl.CostEstimate(flops=1024, bytes_accessed=1024, transcendentals=0)


class Cube:
    def __init__(self, n, orders):
        cores = len(orders)
        self.n, self.orders = n, orders
        self.bits = n.bit_length() - 1
        self.perms = [
            [
                (p * cores + e, (p ^ (1 << self.orders[e][h])) * cores + e)
                for p in range(n)
                for e in range(cores)
            ]
            for h in range(self.bits)
        ]
        self.masks = [
            [
                sum(((i >> (self.bits - 1 - h)) & 1) << self.orders[e][h] for h in range(self.bits))
                for i in range(n)
            ]
            for e in range(cores)
        ]
        self.core = lax.axis_index("ex")
        mine = jnp.array(self.masks, jnp.int32)[self.core]
        self.blocks = jnp.bitwise_xor(lax.axis_index("param"), mine)

    def partners(self, e, i):
        return [p ^ self.masks[e][i] for p in range(self.n)]

    def swap(self, value, hop):
        return lax.ppermute(value, BOTH, self.perms[hop])


def product_kernel(with_top, blocks_ref, g_ref, p_ref, *refs):
    outs = refs[len(refs) - 1 - with_top :]
    value = jnp.dot(g_ref[...], p_ref[...], preferred_element_type=F32)
    outs[0][...] = value.astype(outs[0].dtype)
    if with_top:
        outs[1][...] = jnp.broadcast_to(jnp.max(jnp.abs(value), axis=0, keepdims=True), outs[1].shape)


def product(g, projection, blocks, width, dtype, with_top=False, after=()):
    rows, depth = g.shape
    count = blocks.shape[0]
    out_shape = [jax.ShapeDtypeStruct((rows, count * width), dtype)]
    out_specs = [pl.BlockSpec((rows, width), lambda i, b: (0, i))]
    if with_top:
        out_shape.append(jax.ShapeDtypeStruct((8, count * width), F32))
        out_specs.append(pl.BlockSpec((8, width), lambda i, b: (0, i)))
    return pl.pallas_call(
        functools.partial(product_kernel, with_top),
        grid_spec=pltpu.PrefetchScalarGridSpec(
            num_scalar_prefetch=1,
            grid=(count,),
            in_specs=[
                pl.BlockSpec(memory_space=pltpu.VMEM),
                pl.BlockSpec((depth, width), lambda i, b: (0, b[i])),
            ]
            + [pl.BlockSpec(memory_space=pl.ANY)] * len(after),
            out_specs=out_specs,
        ),
        out_shape=out_shape,
        compiler_params=pltpu.CompilerParams(vmem_limit_bytes=28 * 2**20),
        cost_estimate=LIGHT,
    )(blocks, g, projection, *after)


def fold_kernel(blocks_ref, target_ref, inverse_ref, out_ref):
    count = blocks_ref.shape[0]
    width = target_ref.shape[1] // count
    total = None
    for i in range(count):
        rows = pl.ds(pl.multiple_of(blocks_ref[i] * width, width), width)
        term = jnp.dot(
            target_ref[:, i * width : (i + 1) * width],
            inverse_ref[rows, :],
            preferred_element_type=F32,
        )
        total = term if total is None else total + term
    out_ref[...] = total.astype(out_ref.dtype)


def fold(target, inverse, blocks):
    rows, columns = target.shape[0], inverse.shape[1]
    vmem = pl.BlockSpec(memory_space=pltpu.VMEM)
    return pl.pallas_call(
        fold_kernel,
        in_specs=[pl.BlockSpec(memory_space=pltpu.SMEM), vmem, vmem],
        out_specs=vmem,
        out_shape=jax.ShapeDtypeStruct((rows, columns), BF16),
        compiler_params=pltpu.CompilerParams(vmem_limit_bytes=16 * 2**20),
        cost_estimate=LIGHT,
    )(blocks, target, inverse)


def score_kernel(scale, count, order_ref, own_ref, got_ref, *refs):
    train, outs, (folded_ref, placed_ref) = refs[: -2 - count], refs[-2 - count : -2], refs[-2:]
    rows = own_ref.shape[0]
    folded_ref[:rows] = own_ref[...]
    folded_ref[rows:] = got_ref[...]
    height = 2 * rows // count
    for i in range(count):
        source = pl.ds(pl.multiple_of(order_ref[i] * height, height), height)
        placed_ref[i * height : (i + 1) * height] = folded_ref[source, :]
    folded = placed_ref[...]
    width = train[0].shape[1]
    total = None
    for c in range(len(train) // 2):
        value = train[2 * c][...] + train[2 * c + 1][...].astype(F32)
        high = value.astype(BF16)
        low = (value - high.astype(F32)).astype(BF16)
        for part in (high, low):
            term = lax.dot_general(
                folded[:, c * width : (c + 1) * width],
                part,
                (((1,), (1,)), ((), ())),
                preferred_element_type=F32,
            )
            total = term if total is None else total + term
    total = total * scale
    for i in range(count):
        outs[i][...] = total[i * height : (i + 1) * height].astype(outs[i].dtype)


def score_terms(own, got, train, order, scale):
    rows, columns = own.shape
    count = order.shape[0]
    vmem = pl.BlockSpec(memory_space=pltpu.VMEM)
    shape = (2 * rows // count, train[0].shape[0])
    return pl.pallas_call(
        functools.partial(score_kernel, scale, count),
        in_specs=[pl.BlockSpec(memory_space=pltpu.SMEM)] + [vmem] * (2 + len(train)),
        out_specs=[vmem] * count,
        out_shape=[jax.ShapeDtypeStruct(shape, BF16 if i else F32) for i in range(count)],
        scratch_shapes=[pltpu.VMEM((2 * rows, columns), BF16)] * 2,
        cost_estimate=LIGHT,
        compiler_params=pltpu.CompilerParams(vmem_limit_bytes=16 * 2**20),
    )(order, own, got, *train)


def exponent(top):
    k = jnp.ceil(jnp.log2(jnp.maximum(top, 1e-37)))
    return jnp.clip(k, -110.0, 100.0)


def pack(value, k):
    tail = jnp.broadcast_to(k, (SCALE_ROWS, k.shape[1]))
    return jnp.concatenate([value * jnp.exp2(14.0 - k), tail], axis=0).astype(jnp.float16)


def unpack(message):
    rows = message.shape[0] - SCALE_ROWS
    k = message[rows:].astype(F32)[:1]
    return message[:rows].astype(F32) * jnp.exp2(k - 14.0), k


def halves(value):
    middle = value.shape[1] // 2
    return value[:, :middle], value[:, middle:]


STEPS = (
    "TS", "sT0", "TK", "dT0", "sT1", "Sb", "dT1", "sT2", "sB0", "Kb", "dT2", "sG0", "dB0", "sB1", "Sa", "sA0", "dG0", "sG1", "Ka", "dB1", "dG1", "sG2", "dA0", "sA1", "sB2", "dA1", "sA2", "dG2", "F", "sE0", "dE0", "dB2", "dA2", "SC",
)
AXES = {"T": ("lxh", "xhl"), "L": ("xlh", "lxh"), "A": ("lxh", "xhl"), "B": ("xhl", "lxh")}


def on_device(n, cores, g_train, g_target, projection, kernel_inv):
    features = projection.shape[1]
    width = features // n
    scale = 1.0 / math.sqrt(features)
    swap_cores = [(e, e ^ 1) for e in range(cores)]
    half = n // 2
    cubes = {unit: Cube(n, [["xlh".index(c) for c in axes] for axes in AXES[unit]]) for unit in AXES}
    hops = cubes["T"].bits
    last = []

    def ordered(*values):
        return lax.optimization_barrier((*values, *last))[: len(values)]

    def done(value):
        last[:] = [value]
        return value

    made, moving = {}, {}

    def run(step):
        kind, unit = step[0], step[1:2].upper()
        hop = int(step[2]) if len(step) == 3 else None
        if step in ("TS", "TK"):
            cube = cubes["T"]
            (blocks,) = ordered(cube.blocks[half:] if step == "TS" else cube.blocks[:half])
            value, top = product(g_target, projection, blocks, width, F32, with_top=True)
            made[step] = done(value), exponent(top[:1])
        elif step in ("Sa", "Ka", "Sb", "Kb"):
            blocks = cubes[unit].blocks * 2 + "AB".index(unit)
            blocks, dtype = (blocks[half:], BF16) if kind == "S" else (blocks[:half], F32)
            (blocks,) = ordered(blocks)
            made[step] = done(product(g_train, projection, blocks, width // 2, dtype)[0])
        elif step == "F":
            (target,) = ordered(moving["G"])
            made["F"] = done(fold(target, kernel_inv, cubes["T"].blocks))
        elif step == "SC":
            order = jnp.bitwise_xor(cubes["L"].blocks, half * cubes["L"].core)
            (order,) = ordered(order)
            train = [term for part in "AB" for term in moving[part]]
            made["SC"] = score_terms(made["F"], moving["E"], train, order, scale)
        elif unit == "T" and kind == "s":
            if hop == 0:
                kept, (value, k) = None, made["TS"]
            else:
                (keep, value), (keep_k, k) = map(halves, moving["T"])
                kept = keep, keep_k
            (value,) = ordered(value)
            message = done(pack(value, k))
            moving["T"] = kept, cubes["T"].swap(message, hop)
        elif unit == "T":
            kept, got = moving["T"]
            value, k = made["TK"] if hop == 0 else kept
            (got,) = ordered(got)
            got, other = unpack(got)
            moving["T"] = done(value + got), jnp.maximum(k, other) + 1.0
            if hop == hops - 1:
                moving["G"] = done(moving["T"][0].astype(BF16))
        elif unit == "G" and kind == "s":
            (value,) = ordered(moving["G"])
            moving["G"] = value, cubes["T"].swap(done(value), hops - 1 - hop)
        elif unit == "G":
            value, got = moving["G"]
            (got,) = ordered(got)
            moving["G"] = done(jnp.concatenate([value, got], axis=1))
        elif unit == "E" and kind == "s":
            moving["E"] = lax.ppermute(made["F"], "ex", swap_cores)
        elif unit == "E":
            pass
        elif kind == "s":
            if hop == 0:
                keep, send = None, made["S" + unit.lower()]
            else:
                keep, send = halves(moving[unit])
            (send,) = ordered(send)
            send = done(send.astype(BF16))
            moving[unit] = keep, cubes[unit].swap(send, hop)
        else:
            keep, got = moving[unit]
            keep = made["K" + unit.lower()] if hop == 0 else keep
            (got,) = ordered(got)
            if hop == hops - 1:
                moving[unit] = keep, got
            else:
                moving[unit] = done(keep + got.astype(F32))

    for step in STEPS:
        run(step)

    parts = made["SC"]
    value = parts[0]
    for i in reversed(range(1, n)):
        pairs = [
            (p * cores + e, p_to * cores + e)
            for e in range(cores)
            for p, p_to in enumerate(cubes["L"].partners(e, i))
        ]
        value = value + lax.ppermute(parts[i], BOTH, pairs).astype(F32)
    return value.T


def plain_on_device(g_train, g_target, projection, kernel_inv):
    factor = 1.0 / math.sqrt(projection.shape[1])
    target_part = jnp.dot(g_target, projection, preferred_element_type=F32)
    target_feat = lax.psum_scatter(target_part, "param", scatter_dimension=1, tiled=True)
    target_full = lax.all_gather(target_feat.astype(BF16), "param", axis=1, tiled=True)
    every_target = lax.all_gather(target_full, "ex", axis=0, tiled=True)
    folded = jnp.dot(every_target, kernel_inv, preferred_element_type=F32).astype(BF16)
    train_part = jnp.dot(g_train, projection, preferred_element_type=F32)
    train_feat = lax.psum_scatter(train_part, "param", scatter_dimension=1, tiled=True)
    terms = jnp.dot(train_feat, folded.astype(F32).T, precision=lax.Precision.HIGHEST)
    return lax.psum_scatter(terms * factor, "param", scatter_dimension=1, tiled=True)


def solution(mesh):
    placed = (
        P(("groups", "ex"), "param"),
        P(("groups", "ex"), "param"),
        P("param", None),
        P("groups", "param"),
    )
    n, cores = mesh.shape["param"], mesh.shape["ex"]

    def body(g_train, g_target, projection, kernel_inv):
        whole_blocks = n == 8 and cores == 2 and (projection.shape[1] // n) % 256 == 0
        form = functools.partial(on_device, n, cores) if whole_blocks else plain_on_device
        return form(g_train, g_target, projection, kernel_inv)

    return jax.shard_map(
        body,
        mesh=mesh,
        in_specs=placed,
        out_specs=P(("groups", "ex"), "param"),
        check_vma=False,
    )
```
